32 devices in a mesh: row: 8 (over y, x, core), col: 4 (over z).
Axes of the slice: x: 2, y: 2, z: 4, core: 2. Of those that a mesh axis runs over, the one named last changes fastest.
Arguments:
- eigvecs: float32 [38400, 2560], P('row', 'col'), may hold values from -6 to 6
- panels: float32 [2, 38400, 128], P(None, 'row', 'col'), may hold values from -0.125 to 0.125
- factors: float32 [2, 128, 128], replicated, may hold values from -1 to 1, as said below
Outputs:
- rotated: float32 [38400, 2560], P('row', 'col')
The draws below stay inside these ranges and needn't reach their ends.
Inputs may be any that keep to these rules, and one draw needn't show every extreme that they name: `factors`: each factor is upper triangular with a positive diagonal.
All inputs are finite; a program needn't handle non-finite values.
Results may differ from the reference program's by a relative error of at most 0.0001.
Values sent between devices are 32-bit elements; how exact they have to be, the bound alone decides.
A program may use at most 64 MiB of HBM per device.

```python
import jax
import jax.numpy as jnp
from jax import lax

M = 2560
NB = 128
PANELS = 2
N = 38400


def draw_factors(key, part):
    key = jax.random.fold_in(key, 5)
    key_diag, key_off = jax.random.split(key)
    diag = jax.random.uniform(key_diag, (PANELS, NB), jnp.float32, 0.08, 0.17)
    off = 0.008 * jax.random.normal(key_off, (PANELS, NB, NB), jnp.float32)
    rows = jnp.arange(NB)[:, None]
    cols = jnp.arange(NB)[None, :]
    upper = (cols > rows).astype(jnp.float32)
    eye = (cols == rows).astype(jnp.float32)
    return off * upper[None] + diag[:, :, None] * eye[None]


def shard_levels(key, extent, cuts, least, top_value):
    loudness, own = 1.0, jax.random.fold_in(key, 6)
    for position, parts in cuts:
        steps = jnp.exp(jax.random.uniform(jax.random.fold_in(own, position), (parts,), jnp.float32, least / len(cuts), top_value / len(cuts)))
        loudness = loudness * jnp.repeat(steps, extent[position] // parts).reshape([-1 if axis == position else 1 for axis in range(len(extent))])
    return loudness


def bell_draw(key, extent, scale, most, cuts=(), dtype=jnp.bfloat16):
    values = jax.random.normal(key, extent, jnp.float32) * scale
    if len(cuts) > 0:
        values = shard_levels(key, extent, cuts, -0.22, 0.18) * values
    return jnp.clip(values, min=-most, max=most).astype(dtype)


def setup_inputs(seed: int = 0) -> dict:
    streams_of = jax.random.split(jax.random.key(seed), 4)
    eigvecs = bell_draw(streams_of[0], (N, M), 1.0, 6.0, ((0, 8), (1, 4)), jnp.float32)
    panels = bell_draw(streams_of[1], (PANELS, N, NB), (N // 16) ** -0.5, 0.125, ((1, 8), (2, 4)), jnp.float32)
    factors = draw_factors(jax.random.fold_in(streams_of[3], 71), 0)
    return dict(eigvecs=eigvecs, panels=panels, factors=factors)


def reference(eigvecs, panels, factors):
    hi = lax.Precision.HIGHEST
    rotated = eigvecs
    for index in range(PANELS):
        vectors = panels[index]
        projection = lax.dot_general(vectors, rotated, (((0,), (0,)), ((), ())), precision=hi, preferred_element_type=jnp.float32)
        scaled = jnp.dot(factors[index], projection, precision=hi, preferred_element_type=jnp.float32)
        rotated = rotated - jnp.dot(vectors, scaled, precision=hi, preferred_element_type=jnp.float32)
    return rotated
```

```python
import functools

import jax
import jax.numpy as jnp
from jax import lax
from jax.experimental import pallas as pl
from jax.experimental.pallas import tpu as pltpu
from jax.sharding import PartitionSpec as P

MESH = pl.DeviceIdType.MESH
PIECE = 16
DEPTH = 768
F32 = jnp.float32
BF16 = jnp.bfloat16


def halves(value):
    high = value.astype(BF16)
    return high, (value - high.astype(F32)).astype(BF16)


def rows_by(left, right):
    return lax.dot_general(left, right, (((1,), (1,)), ((), ())), preferred_element_type=F32)


def plain(left, right):
    return lax.dot_general(left, right, (((1,), (0,)), ((), ())), preferred_element_type=F32)


def exact(left, right):
    return jnp.dot(left, right, precision=lax.Precision.HIGHEST, preferred_element_type=F32)


def gather_kernel(
    peers, line, step, own_ref, x_ref, factors_ref, vh_out, vl_out, sh_ref, sl_ref,
    vt, vh, vl, xh, xl, stage, part0, part1, got0, got1, small, final,
    own_sem, x_sem, out_sem, left_sem, right_sem, recv_sem, put_sem, got_sem,
):
    row, col = lax.axis_index("row"), lax.axis_index("col")
    columns, count = own_ref.shape[1:]
    per = columns // PIECE
    width = x_ref.shape[1]
    panel_columns = vh.shape[1]
    full = count // DEPTH
    parts, gots = (part0, part1), (got0, got1)

    own_copy = pltpu.make_async_copy(own_ref, vt.at[col], own_sem)
    own_copy.start()

    def fetch(block):
        slot = lax.rem(block, 2)
        return pltpu.make_async_copy(x_ref.at[pl.ds(pl.multiple_of(block * step, step), step)], stage.at[slot], x_sem.at[slot])

    fetch(0).start()

    barrier = pltpu.get_barrier_semaphore()
    for offset in range(1, peers):
        pl.semaphore_signal(barrier, inc=1, device_id=(lax.rem(row + offset, peers), col), device_id_type=MESH)

    @pl.when(col > 0)
    def _():
        pl.semaphore_signal(barrier, inc=1, device_id=(row, col - 1), device_id_type=MESH)

    @pl.when(col < line - 1)
    def _():
        pl.semaphore_signal(barrier, inc=1, device_id=(row, col + 1), device_id_type=MESH)

    pl.semaphore_wait(barrier, peers - 1 + jnp.where(col > 0, 1, 0) + jnp.where(col < line - 1, 1, 0))

    def move(source, origin, panel, half, sems, away, target):
        place = pl.ds(pl.multiple_of(half * PIECE, PIECE), PIECE)
        return pltpu.make_async_remote_copy(
            src_ref=source.at[panel, place],
            dst_ref=vt.at[origin, panel, place],
            send_sem=sems.at[away, panel, half],
            recv_sem=recv_sem.at[origin, panel, half],
            device_id=(row, target),
            device_id_type=MESH,
        )

    def own_sends(act):
        for panel in range(2):
            for half in range(per):
                @pl.when(col > 0)
                def _():
                    act(move(own_ref, col, panel, half, left_sem, 0, col - 1))

                @pl.when(col < line - 1)
                def _():
                    act(move(own_ref, col, panel, half, right_sem, 0, col + 1))

    own_sends(lambda copy: copy.start())

    blocks = count // step

    @pl.loop(0, blocks)
    def _(block):
        @pl.when(block + 1 < blocks)
        def _():
            fetch(block + 1).start()

        fetch(block).wait()
        place = pl.ds(pl.multiple_of(block * step, step), step)
        high, low = halves(stage[lax.rem(block, 2)])
        xh[place] = high
        xl[place] = low

    own_copy.wait()

    def process(origin, panel, half):
        index = origin * per + half
        place = pl.ds(pl.multiple_of(index * PIECE, PIECE), PIECE)
        part = parts[panel]
        vt_place = pl.ds(pl.multiple_of(half * PIECE, PIECE), PIECE)
        part[index] = jnp.zeros(part.shape[1:], F32)

        def block(lanes, rows):
            high, low = halves(vt[origin, panel, vt_place, lanes])
            vh[panel, place, lanes] = high
            vl[panel, place, lanes] = low
            both = jnp.concatenate([high, low], axis=0)
            first = plain(both, xh[rows])
            second = plain(high, xl[rows])
            part[index, :, :width] += first[:PIECE] + first[PIECE:] + second
            if panel == 1:
                third = rows_by(both, vh[0, :, lanes])
                fourth = rows_by(high, vl[0, :, lanes])
                part[index, :, width:] += third[:PIECE] + third[PIECE:] + fourth

        @pl.loop(0, full)
        def _(number):
            place = pl.ds(pl.multiple_of(number * DEPTH, DEPTH), DEPTH)
            block(place, place)

        if count % DEPTH:
            rest = pl.ds(full * DEPTH, count - full * DEPTH)
            block(rest, rest)

        @pl.loop(1, peers)
        def _(offset):
            pltpu.make_async_remote_copy(
                src_ref=part.at[index],
                dst_ref=gots[panel].at[index, offset - 1],
                send_sem=put_sem.at[panel, index],
                recv_sem=got_sem.at[panel, index],
                device_id=(lax.rem(row + offset, peers), col),
                device_id_type=MESH,
            ).start()

    def arrivals(panel):
        @pl.loop(1, line)
        def _(away):
            right, left = col + away, col - away

            @pl.loop(0, per)
            def _(half):
                @pl.when(right < line)
                def _():
                    move(own_ref, right, panel, half, left_sem, away, col).wait_recv()

                    @pl.when(col > 0)
                    def _():
                        move(vt.at[right], right, panel, half, left_sem, away, col - 1).start()

                @pl.when(left >= 0)
                def _():
                    move(own_ref, left, panel, half, right_sem, away, col).wait_recv()

                    @pl.when(col < line - 1)
                    def _():
                        move(vt.at[left], left, panel, half, right_sem, away, col + 1).start()

                @pl.when(right < line)
                def _():
                    process(right, panel, half)

                @pl.when(left >= 0)
                def _():
                    process(left, panel, half)

    def own_pieces(panel):
        @pl.loop(0, per)
        def _(half):
            process(col, panel, half)

    def save(panel):
        return (
            pltpu.make_async_copy(vh.at[panel], vh_out.at[panel], out_sem.at[panel, 0]),
            pltpu.make_async_copy(vl.at[panel], vl_out.at[panel], out_sem.at[panel, 1]),
        )

    def collect(panel, keep):
        part, got = parts[panel], gots[panel]

        @pl.loop(0, line * per)
        def _(index):
            pltpu.make_async_copy(got.at[index], got.at[index], got_sem.at[panel, index]).wait()
            total = part[index]
            for offset in range(peers - 1):
                total = total + got[index, offset]
            keep[pl.ds(pl.multiple_of(index * PIECE, PIECE), PIECE)] = total

    def emit(panel, scaled):
        high, low = halves(scaled)
        sh_ref[panel] = high
        sl_ref[panel] = low

    own_pieces(0)
    arrivals(0)
    for copy in save(0):
        copy.start()
    own_pieces(1)
    collect(0, small)
    scaled = exact(factors_ref[0], small[...])
    emit(0, scaled)
    small[...] = scaled
    arrivals(1)
    for copy in save(1):
        copy.start()

    collect(1, final)
    projection = final[:, :width] - exact(final[:, width:], small[...])
    emit(1, exact(factors_ref[1], projection))

    own_sends(lambda copy: copy.wait_send())
    for panel in range(2):
        @pl.loop(1, line)
        def _(away):
            @pl.loop(0, per)
            def _(half):
                @pl.when(jnp.logical_and(col + away < line, col > 0))
                def _():
                    move(own_ref, col + away, panel, half, left_sem, away, col - 1).wait_send()

                @pl.when(jnp.logical_and(col - away >= 0, col < line - 1))
                def _():
                    move(own_ref, col - away, panel, half, right_sem, away, col + 1).wait_send()

        @pl.loop(0, line * per)
        def _(index):
            got = gots[panel]
            pltpu.make_async_copy(got.at[index], got.at[index], put_sem.at[panel, index]).wait()

        for copy in save(panel):
            copy.wait()


def update_kernel(x_ref, vh_ref, vl_ref, sh_ref, sl_ref, out_ref):
    def product(left, right):
        return lax.dot_general(left, right, (((0,), (0,)), ((), ())), preferred_element_type=F32)

    high = vh_ref[...]
    out_ref[...] = x_ref[...] - (
        product(high, sh_ref[...]) + product(vl_ref[...], sh_ref[...]) + product(high, sl_ref[...])
    )


def per_device(peers, line, eigvecs, panels, factors):
    count, width = eigvecs.shape
    columns = panels.shape[2]
    total = columns * line
    per = columns // PIECE
    step = 480 if count % 480 == 0 else PIECE
    own = jnp.swapaxes(panels, 1, 2)
    anywhere = pl.BlockSpec(memory_space=pl.ANY)
    inside = pl.BlockSpec(memory_space=pltpu.VMEM)
    pieces = line * per
    wide = width + total
    vh, vl, sh, sl = pl.pallas_call(
        functools.partial(gather_kernel, peers, line, step),
        out_shape=(
            jax.ShapeDtypeStruct((2, total, count), BF16),
            jax.ShapeDtypeStruct((2, total, count), BF16),
            jax.ShapeDtypeStruct((2, total, width), BF16),
            jax.ShapeDtypeStruct((2, total, width), BF16),
        ),
        in_specs=[anywhere, anywhere, inside],
        out_specs=(anywhere, anywhere, inside, inside),
        scratch_shapes=[
            pltpu.VMEM((line, 2, columns, count), F32),
            pltpu.VMEM((2, total, count), BF16),
            pltpu.VMEM((2, total, count), BF16),
            pltpu.VMEM((count, width), BF16),
            pltpu.VMEM((count, width), BF16),
            pltpu.VMEM((2, step, width), F32),
            pltpu.VMEM((pieces, PIECE, width), F32),
            pltpu.VMEM((pieces, PIECE, wide), F32),
            pltpu.VMEM((pieces, peers - 1, PIECE, width), F32),
            pltpu.VMEM((pieces, peers - 1, PIECE, wide), F32),
            pltpu.VMEM((total, width), F32),
            pltpu.VMEM((total, wide), F32),
            pltpu.SemaphoreType.DMA,
            pltpu.SemaphoreType.DMA((2,)),
            pltpu.SemaphoreType.DMA((2, 2)),
            pltpu.SemaphoreType.DMA((line, 2, per)),
            pltpu.SemaphoreType.DMA((line, 2, per)),
            pltpu.SemaphoreType.DMA((line, 2, per)),
            pltpu.SemaphoreType.DMA((2, pieces)),
            pltpu.SemaphoreType.DMA((2, pieces)),
        ],
        compiler_params=pltpu.CompilerParams(
            collective_id=0, has_side_effects=True, vmem_limit_bytes=44 * 1024 * 1024
        ),
        name="gather_project",
    )(own, eigvecs, factors)
    vh, vl, sh, sl = (array.reshape(2 * total, array.shape[2]) for array in (vh, vl, sh, sl))
    rows = min(640, count)
    tall = pl.BlockSpec((rows, width), lambda number: (number, 0))
    flat = pl.BlockSpec((2 * total, rows), lambda number: (0, number))
    fixed = pl.BlockSpec((2 * total, width), lambda number: (0, 0))
    return pl.pallas_call(
        update_kernel,
        out_shape=jax.ShapeDtypeStruct((count, width), F32),
        grid=(pl.cdiv(count, rows),),
        in_specs=[tall, flat, flat, fixed, fixed],
        out_specs=tall,
        compiler_params=pltpu.CompilerParams(vmem_limit_bytes=32 * 1024 * 1024),
        name="update",
    )(eigvecs, vh, vl, sh, sl)


def solution(mesh):
    return jax.shard_map(
        functools.partial(per_device, mesh.shape["row"], mesh.shape["col"]),
        mesh=mesh,
        in_specs=(P("row", "col"), P(None, "row", "col"), P()),
        out_specs=P("row", "col"),
        check_vma=False,
    )
```

```python
import functools

import jax
import jax.numpy as jnp
from jax import lax
from jax.experimental import pallas as pl
from jax.experimental.pallas import tpu as pltpu
from jax.sharding import PartitionSpec as P

MESH = pl.DeviceIdType.MESH
PIECE = 16
DEPTH = 768
F32 = jnp.float32
BF16 = jnp.bfloat16


def halves(value):
    high = value.astype(BF16)
    return high, (value - high.astype(F32)).astype(BF16)


def rows_by(left, right):
    return lax.dot_general(left, right, (((1,), (1,)), ((), ())), preferred_element_type=F32)


def plain(left, right):
    return lax.dot_general(left, right, (((1,), (0,)), ((), ())), preferred_element_type=F32)


def across(left, right):
    return lax.dot_general(left, right, (((0,), (0,)), ((), ())), preferred_element_type=F32)


def spans(count):
    return [(start, min(DEPTH, count - start)) for start in range(0, count, DEPTH)]


def exact(left, right):
    return jnp.dot(left, right, precision=lax.Precision.HIGHEST, preferred_element_type=F32)


def gather_kernel(
    peers, line, own_ref, x_ref, factors_hbm, x1, vh1, vl1, sh_ref, sl_ref,
    vt, vh0, vl0, xh, xl, part0, part1, part2, got0, got1, got2, scaled, final, gram, factors_ref,
    own_sem, factors_sem, x_sem, left_sem, right_sem, recv_sem, put_sem, got_sem,
):
    row, col = lax.axis_index("row"), lax.axis_index("col")
    columns, count = own_ref.shape[1:]
    per = columns // PIECE
    early = per // 2
    full, rest = count // DEPTH, count % DEPTH
    highs, lows = (vh0, vh1), (vl0, vl1)
    parts, gots = (part0, part1, part2), (got0, got1, got2)

    own_copy = pltpu.make_async_copy(own_ref, vt.at[col], own_sem)
    factors_copy = pltpu.make_async_copy(factors_hbm, factors_ref, factors_sem)

    def fetch(number):
        start, size = spans(count)[number]
        place = pl.ds(start, size)
        return pltpu.make_async_copy(x_ref.at[place], x1.at[place], x_sem.at[number])

    barrier = pltpu.get_barrier_semaphore()
    for offset in range(1, peers):
        pl.semaphore_signal(barrier, inc=1, device_id=(lax.rem(row + offset, peers), col), device_id_type=MESH)

    @pl.when(col > 0)
    def _():
        pl.semaphore_signal(barrier, inc=1, device_id=(row, col - 1), device_id_type=MESH)

    @pl.when(col < line - 1)
    def _():
        pl.semaphore_signal(barrier, inc=1, device_id=(row, col + 1), device_id_type=MESH)

    own_copy.start()
    for number in range(len(spans(count))):
        fetch(number).start()
    factors_copy.start()
    pl.semaphore_wait(barrier, peers - 1 + jnp.where(col > 0, 1, 0) + jnp.where(col < line - 1, 1, 0))

    def move(source, origin, panel, half, sems, away, target):
        place = pl.ds(pl.multiple_of(half * PIECE, PIECE), PIECE)
        return pltpu.make_async_remote_copy(
            src_ref=source.at[panel, place],
            dst_ref=vt.at[origin, panel, place],
            send_sem=sems.at[away, panel, half],
            recv_sem=recv_sem.at[origin, panel, half],
            device_id=(row, target),
            device_id_type=MESH,
        )

    def own_left(panel, half):
        return move(own_ref, col, panel, half, left_sem, 0, col - 1)

    def own_right(panel, half):
        return move(own_ref, col, panel, half, right_sem, 0, col + 1)

    firsts = [(0, half) for half in range(per)] + [(1, half) for half in range(early)]
    lates = [(1, half) for half in range(early, per)]

    for panel, half in firsts:
        @pl.when(col > 0)
        def _():
            own_left(panel, half).start()

        @pl.when(col < line - 1)
        def _():
            own_right(panel, half).start()

    for panel, half in lates:
        @pl.when(col == line - 1)
        def _():
            own_left(panel, half).start()

        @pl.when(col == 0)
        def _():
            own_right(panel, half).start()

    for number, (start, size) in enumerate(spans(count)):
        fetch(number).wait()

        @pl.loop(0, size // 64)
        def _(block):
            place = pl.ds(pl.multiple_of(start + block * 64, 64), 64)
            high, low = halves(x1[place])
            xh[place] = high
            xl[place] = low

    own_copy.wait()
    factors_copy.wait()

    def spread(kind, index):
        @pl.loop(1, peers)
        def _(offset):
            pltpu.make_async_remote_copy(
                src_ref=parts[kind].at[index],
                dst_ref=gots[kind].at[index, offset - 1],
                send_sem=put_sem.at[kind, index],
                recv_sem=got_sem.at[kind, index],
                device_id=(lax.rem(row + offset, peers), col),
                device_id_type=MESH,
            ).start()

    def process(origin, panel, half, pieces, project=True, overlap=False):
        index = origin * per + half
        size = pieces * PIECE
        place = pl.ds(pl.multiple_of(index * PIECE, PIECE), size)
        source = pl.ds(pl.multiple_of(half * PIECE, PIECE), size)

        def add(kind, value):
            for piece in range(pieces):
                parts[kind][index + piece] += value[piece * PIECE : (piece + 1) * PIECE]

        for piece in range(pieces):
            if project:
                parts[panel][index + piece] = jnp.zeros(parts[panel].shape[1:], F32)
            if overlap:
                parts[2][index + piece] = jnp.zeros(parts[2].shape[1:], F32)

        def block(lanes):
            if project:
                high, low = halves(vt[origin, panel, source, lanes])
                highs[panel][place, lanes] = high
                lows[panel][place, lanes] = low
            else:
                high, low = highs[panel][place, lanes], lows[panel][place, lanes]
            both = jnp.concatenate([high, low], axis=0)
            if project:
                first = plain(both, xh[lanes])
                add(panel, first[:size] + first[size:] + plain(high, xl[lanes]))
            if overlap:
                third = rows_by(both, vh0[:, lanes])
                add(2, third[:size] + third[size:] + rows_by(high, vl0[:, lanes]))

        @pl.loop(0, full)
        def _(number):
            block(pl.ds(pl.multiple_of(number * DEPTH, DEPTH), DEPTH))

        if rest:
            block(pl.ds(full * DEPTH, rest))

        for piece in range(pieces):
            if project:
                spread(panel, index + piece)
            if overlap:
                spread(2, index + piece)

    def sides(away, act):
        @pl.when(col + away < line)
        def _():
            act(col + away)

        @pl.when(col - away >= 0)
        def _():
            act(col - away)

    def receive(panel, away, half):
        right, left = col + away, col - away

        @pl.when(right < line)
        def _():
            move(own_ref, right, panel, half, left_sem, away, col).wait_recv()

            @pl.when(col > 0)
            def _():
                move(vt.at[right], right, panel, half, left_sem, away, col - 1).start()

        @pl.when(left >= 0)
        def _():
            move(own_ref, left, panel, half, right_sem, away, col).wait_recv()

            @pl.when(col < line - 1)
            def _():
                move(vt.at[left], left, panel, half, right_sem, away, col + 1).start()

    def receive_all(panel, away):
        for half in range(per):
            receive(panel, away, half)

    def collect(kind, keep):
        part, got = parts[kind], gots[kind]

        @pl.loop(0, line * per)
        def _(index):
            pltpu.make_async_copy(got.at[index], got.at[index], got_sem.at[kind, index]).wait()
            total = part[index]
            for offset in range(peers - 1):
                total = total + got[index, offset]
            keep[pl.ds(pl.multiple_of(index * PIECE, PIECE), PIECE)] = total

    process(col, 0, 0, per)

    @pl.loop(1, line)
    def _(away):
        receive_all(0, away)

        for panel, half in lates:
            @pl.when(jnp.logical_and(col + away == line - 1, col > 0))
            def _():
                own_left(panel, half).start()

            @pl.when(jnp.logical_and(col - away == 0, col < line - 1))
            def _():
                own_right(panel, half).start()

        sides(away, lambda origin: process(origin, 0, 0, per))

        @pl.when(away == 1)
        def _():
            process(col, 1, 0, per)

    def apply_first():
        collect(0, scaled)
        value = exact(factors_ref[0], scaled[...])
        scaled[...] = value
        high, low = halves(value)
        sh_ref[...] = high
        sl_ref[...] = low

        def block(lanes):
            upper, lower = vh0[:, lanes], vl0[:, lanes]
            both = jnp.concatenate([upper, lower], axis=0)
            twice = jnp.concatenate([sh_ref[...], sh_ref[...]], axis=0)
            x1[lanes] = x1[lanes] - (across(both, twice) + across(upper, sl_ref[...]))

        @pl.loop(0, full)
        def _(number):
            block(pl.ds(pl.multiple_of(number * DEPTH, DEPTH), DEPTH))

        if rest:
            block(pl.ds(full * DEPTH, rest))

        process(col, 1, 0, per, project=False, overlap=True)

    for away in range(1, line - 1):
        receive_all(1, away)
        if away == 1:
            sides(away, lambda origin: process(origin, 1, 0, per))
            apply_first()
            sides(away, lambda origin: process(origin, 1, 0, per, project=False, overlap=True))
        else:
            sides(away, lambda origin: process(origin, 1, 0, per, overlap=True))
    if line == 2:
        apply_first()
    for half in range(per):
        receive(1, line - 1, half)
        sides(line - 1, lambda origin: process(origin, 1, half, 1, overlap=True))

    collect(2, gram)
    collect(1, final)
    projection = final[...] - exact(gram[...], scaled[...])
    high, low = halves(exact(factors_ref[1], projection))
    sh_ref[...] = high
    sl_ref[...] = low

    for panel in range(2):
        for half in range(per):
            @pl.when(col > 0)
            def _():
                own_left(panel, half).wait_send()

            @pl.when(col < line - 1)
            def _():
                own_right(panel, half).wait_send()

        @pl.loop(1, line)
        def _(away):
            @pl.loop(0, per)
            def _(half):
                @pl.when(jnp.logical_and(col + away < line, col > 0))
                def _():
                    move(own_ref, col + away, panel, half, left_sem, away, col - 1).wait_send()

                @pl.when(jnp.logical_and(col - away >= 0, col < line - 1))
                def _():
                    move(own_ref, col - away, panel, half, right_sem, away, col + 1).wait_send()

    for kind in range(3):
        got = gots[kind]

        @pl.loop(0, line * per)
        def _(index):
            pltpu.make_async_copy(got.at[index], got.at[index], put_sem.at[kind, index]).wait()


def update_kernel(x_ref, vh_ref, vl_ref, sh_ref, sl_ref, out_ref, stage, sems):
    count = x_ref.shape[0]
    twice = jnp.concatenate([sh_ref[...], sh_ref[...]], axis=0)

    def put(number):
        start, size = spans(count)[number]
        return pltpu.make_async_copy(stage.at[number % 2, pl.ds(0, size)], out_ref.at[pl.ds(start, size)], sems.at[number % 2])

    numbers = range(len(spans(count)))
    for number in numbers:
        start, size = spans(count)[number]
        place = pl.ds(start, size)
        if number >= 2:
            put(number - 2).wait()
        upper = vh_ref[:, place]
        both = jnp.concatenate([upper, vl_ref[:, place]], axis=0)
        stage[number % 2, :size] = x_ref[place] - (across(both, twice) + across(upper, sl_ref[...]))
        put(number).start()
    for number in numbers[-2:]:
        put(number).wait()


def per_device(peers, line, eigvecs, panels, factors):
    count, width = eigvecs.shape
    columns = panels.shape[2]
    total = columns * line
    per = columns // PIECE
    own = jnp.swapaxes(panels, 1, 2)
    outside = pl.BlockSpec(memory_space=pltpu.HBM)
    inside = pl.BlockSpec(memory_space=pltpu.VMEM)
    pieces = line * per
    held = pl.pallas_call(
        functools.partial(gather_kernel, peers, line),
        out_shape=(
            jax.ShapeDtypeStruct((count, width), F32),
            jax.ShapeDtypeStruct((total, count), BF16),
            jax.ShapeDtypeStruct((total, count), BF16),
            jax.ShapeDtypeStruct((total, width), BF16),
            jax.ShapeDtypeStruct((total, width), BF16),
        ),
        in_specs=[outside] * 3,
        out_specs=(inside,) * 5,
        scratch_shapes=[
            pltpu.VMEM((line, 2, columns, count), F32),
            pltpu.VMEM((total, count), BF16),
            pltpu.VMEM((total, count), BF16),
            pltpu.VMEM((count, width), BF16),
            pltpu.VMEM((count, width), BF16),
            pltpu.VMEM((pieces, PIECE, width), F32),
            pltpu.VMEM((pieces, PIECE, width), F32),
            pltpu.VMEM((pieces, PIECE, total), F32),
            pltpu.VMEM((pieces, peers - 1, PIECE, width), F32),
            pltpu.VMEM((pieces, peers - 1, PIECE, width), F32),
            pltpu.VMEM((pieces, peers - 1, PIECE, total), F32),
            pltpu.VMEM((total, width), F32),
            pltpu.VMEM((total, width), F32),
            pltpu.VMEM((total, total), F32),
            pltpu.VMEM(factors.shape, F32),
            pltpu.SemaphoreType.DMA,
            pltpu.SemaphoreType.DMA,
            pltpu.SemaphoreType.DMA((len(spans(count)),)),
            pltpu.SemaphoreType.DMA((line, 2, per)),
            pltpu.SemaphoreType.DMA((line, 2, per)),
            pltpu.SemaphoreType.DMA((line, 2, per)),
            pltpu.SemaphoreType.DMA((3, pieces)),
            pltpu.SemaphoreType.DMA((3, pieces)),
        ],
        compiler_params=pltpu.CompilerParams(
            collective_id=0, has_side_effects=True, vmem_limit_bytes=30 * 1024 * 1024
        ),
        name="gather_project",
    )(*(pltpu.with_memory_space_constraint(array, pltpu.HBM) for array in (own, eigvecs, factors)))
    return pl.pallas_call(
        update_kernel,
        out_shape=jax.ShapeDtypeStruct((count, width), F32),
        in_specs=[inside] * 5,
        out_specs=outside,
        scratch_shapes=[pltpu.VMEM((2, DEPTH, width), F32), pltpu.SemaphoreType.DMA((2,))],
        compiler_params=pltpu.CompilerParams(vmem_limit_bytes=24 * 1024 * 1024),
        name="update",
    )(*held)


def solution(mesh):
    return jax.shard_map(
        functools.partial(per_device, mesh.shape["row"], mesh.shape["col"]),
        mesh=mesh,
        in_specs=(P("row", "col"), P(None, "row", "col"), P()),
        out_specs=P("row", "col"),
        check_vma=False,
    )
```

```python
import functools

import jax
import jax.numpy as jnp
from jax import lax
from jax.experimental import pallas as pl
from jax.experimental.pallas import tpu as pltpu
from jax.sharding import PartitionSpec as P

MESH = pl.DeviceIdType.MESH
PIECE = 16
DEPTH = 768
F32 = jnp.float32
BF16 = jnp.bfloat16


def halves(value):
    high = value.astype(BF16)
    return high, (value - high.astype(F32)).astype(BF16)


def plain(left, right):
    return lax.dot_general(left, right, (((1,), (0,)), ((), ())), preferred_element_type=F32)


def across(left, right):
    return lax.dot_general(left, right, (((0,), (0,)), ((), ())), preferred_element_type=F32)


def spans(count):
    return [(start, min(DEPTH, count - start)) for start in range(0, count, DEPTH)]


def exact(left, right):
    return jnp.dot(left, right, precision=lax.Precision.HIGHEST, preferred_element_type=F32)


def gather_kernel(
    peers, line, own_ref, x_ref, factors_hbm, x1, vh1, vl1, sh_ref, sl_ref,
    vt, vh0, vl0, xh, xl, part0, part1, got0, got1, scaled, factors_ref,
    own_sem, factors_sem, x_sem, left_sem, right_sem, recv_sem, put_sem, got_sem,
):
    row, col = lax.axis_index("row"), lax.axis_index("col")
    columns, count = own_ref.shape[1:]
    per = columns // PIECE
    early = per // 2
    full, rest = count // DEPTH, count % DEPTH
    highs, lows = (vh0, vh1), (vl0, vl1)
    parts, gots = (part0, part1), (got0, got1)

    own_copy = pltpu.make_async_copy(own_ref, vt.at[col], own_sem)
    factors_copy = pltpu.make_async_copy(factors_hbm, factors_ref, factors_sem)

    def fetch(number):
        start, size = spans(count)[number]
        place = pl.ds(start, size)
        return pltpu.make_async_copy(x_ref.at[place], x1.at[place], x_sem.at[number])

    barrier = pltpu.get_barrier_semaphore()
    for offset in range(1, peers):
        pl.semaphore_signal(barrier, inc=1, device_id=(lax.rem(row + offset, peers), col), device_id_type=MESH)

    @pl.when(col > 0)
    def _():
        pl.semaphore_signal(barrier, inc=1, device_id=(row, col - 1), device_id_type=MESH)

    @pl.when(col < line - 1)
    def _():
        pl.semaphore_signal(barrier, inc=1, device_id=(row, col + 1), device_id_type=MESH)

    own_copy.start()
    for number in range(len(spans(count))):
        fetch(number).start()
    factors_copy.start()
    pl.semaphore_wait(barrier, peers - 1 + jnp.where(col > 0, 1, 0) + jnp.where(col < line - 1, 1, 0))

    def move(source, origin, panel, half, sems, away, target):
        place = pl.ds(pl.multiple_of(half * PIECE, PIECE), PIECE)
        return pltpu.make_async_remote_copy(
            src_ref=source.at[panel, place],
            dst_ref=vt.at[origin, panel, place],
            send_sem=sems.at[away, panel, half],
            recv_sem=recv_sem.at[origin, panel, half],
            device_id=(row, target),
            device_id_type=MESH,
        )

    def own_left(panel, half):
        return move(own_ref, col, panel, half, left_sem, 0, col - 1)

    def own_right(panel, half):
        return move(own_ref, col, panel, half, right_sem, 0, col + 1)

    firsts = [(0, half) for half in range(per)] + [(1, half) for half in range(early)]
    lates = [(1, half) for half in range(early, per)]

    for panel, half in firsts:
        @pl.when(col > 0)
        def _():
            own_left(panel, half).start()

        @pl.when(col < line - 1)
        def _():
            own_right(panel, half).start()

    for panel, half in lates:
        @pl.when(col == line - 1)
        def _():
            own_left(panel, half).start()

        @pl.when(col == 0)
        def _():
            own_right(panel, half).start()

    for number, (start, size) in enumerate(spans(count)):
        fetch(number).wait()

        @pl.loop(0, size // 64)
        def _(block):
            place = pl.ds(pl.multiple_of(start + block * 64, 64), 64)
            high, low = halves(x1[place])
            xh[place] = high
            xl[place] = low

    own_copy.wait()
    factors_copy.wait()

    def spread(kind, index):
        @pl.loop(1, peers)
        def _(offset):
            pltpu.make_async_remote_copy(
                src_ref=parts[kind].at[index],
                dst_ref=gots[kind].at[index, offset - 1],
                send_sem=put_sem.at[kind, index],
                recv_sem=got_sem.at[kind, index],
                device_id=(lax.rem(row + offset, peers), col),
                device_id_type=MESH,
            ).start()

    def process(panel, origin, shards, half, pieces):
        index = origin * per + half
        size = shards * pieces * PIECE
        place = pl.ds(pl.multiple_of(index * PIECE, PIECE), size)
        source = pl.ds(pl.multiple_of(half * PIECE, PIECE), pieces * PIECE)
        part = parts[panel]
        number_of = shards * pieces
        part[pl.ds(index, number_of)] = jnp.zeros((number_of,) + part.shape[1:], F32)

        def block(lanes):
            value = vt[pl.ds(origin, shards), panel, source, lanes]
            high, low = halves(value.reshape(size, value.shape[2]))
            highs[panel][place, lanes] = high
            lows[panel][place, lanes] = low
            both = jnp.concatenate([high, low], axis=0)
            first = plain(both, xh[lanes])
            total = first[:size] + first[size:] + plain(high, xl[lanes])
            part[pl.ds(index, number_of)] += total.reshape(number_of, PIECE, total.shape[1])

        @pl.loop(0, full)
        def _(number):
            block(pl.ds(pl.multiple_of(number * DEPTH, DEPTH), DEPTH))

        if rest:
            block(pl.ds(full * DEPTH, rest))

        for piece in range(number_of):
            spread(panel, index + piece)

    def receive(panel, away, half):
        right, left = col + away, col - away

        @pl.when(right < line)
        def _():
            move(own_ref, right, panel, half, left_sem, away, col).wait_recv()

            @pl.when(col > 0)
            def _():
                move(vt.at[right], right, panel, half, left_sem, away, col - 1).start()

        @pl.when(left >= 0)
        def _():
            move(own_ref, left, panel, half, right_sem, away, col).wait_recv()

            @pl.when(col < line - 1)
            def _():
                move(vt.at[left], left, panel, half, right_sem, away, col + 1).start()

    def receive_all(panel, away):
        for half in range(per):
            receive(panel, away, half)

    def collect(kind, keep):
        part, got = parts[kind], gots[kind]

        @pl.loop(0, line * per)
        def _(index):
            pltpu.make_async_copy(got.at[index], got.at[index], got_sem.at[kind, index]).wait()
            total = part[index]
            for offset in range(peers - 1):
                total = total + got[index, offset]
            keep[pl.ds(pl.multiple_of(index * PIECE, PIECE), PIECE)] = total

    @pl.loop(1, line)
    def _(away):
        receive_all(0, away)

        for panel, half in lates:
            @pl.when(jnp.logical_and(col + away == line - 1, col > 0))
            def _():
                own_left(panel, half).start()

            @pl.when(jnp.logical_and(col - away == 0, col < line - 1))
            def _():
                own_right(panel, half).start()

    process(0, 0, line, 0, per)

    def apply_first():
        collect(0, scaled)
        value = exact(factors_ref[0], scaled[...])
        scaled[...] = value
        high, low = halves(value)
        sh_ref[...] = high
        sl_ref[...] = low

        def block(lanes):
            upper, lower = vh0[:, lanes], vl0[:, lanes]
            both = jnp.concatenate([upper, lower], axis=0)
            twice = jnp.concatenate([sh_ref[...], sh_ref[...]], axis=0)
            value = x1[lanes] - (across(both, twice) + across(upper, sl_ref[...]))
            x1[lanes] = value
            high, low = halves(value)
            xh[lanes] = high
            xl[lanes] = low

        @pl.loop(0, full)
        def _(number):
            block(pl.ds(pl.multiple_of(number * DEPTH, DEPTH), DEPTH))

        if rest:
            block(pl.ds(full * DEPTH, rest))

    if line > 2:
        receive_all(1, 1)
    apply_first()
    for away in range(2, line - 1):
        receive_all(1, away)
    top = col == line - 1
    process(1, jnp.where(top, 1, 0), line - 1, 0, per)
    for half in range(per):
        receive(1, line - 1, half)
        process(1, jnp.where(top, 0, line - 1), 1, half, 1)

    collect(1, scaled)
    projection = scaled[...]
    high, low = halves(exact(factors_ref[1], projection))
    sh_ref[...] = high
    sl_ref[...] = low

    for panel in range(2):
        for half in range(per):
            @pl.when(col > 0)
            def _():
                own_left(panel, half).wait_send()

            @pl.when(col < line - 1)
            def _():
                own_right(panel, half).wait_send()

        @pl.loop(1, line)
        def _(away):
            @pl.loop(0, per)
            def _(half):
                @pl.when(jnp.logical_and(col + away < line, col > 0))
                def _():
                    move(own_ref, col + away, panel, half, left_sem, away, col - 1).wait_send()

                @pl.when(jnp.logical_and(col - away >= 0, col < line - 1))
                def _():
                    move(own_ref, col - away, panel, half, right_sem, away, col + 1).wait_send()

    for kind in range(2):
        got = gots[kind]

        @pl.loop(0, line * per)
        def _(index):
            pltpu.make_async_copy(got.at[index], got.at[index], put_sem.at[kind, index]).wait()


def update_kernel(x_ref, vh_ref, vl_ref, sh_ref, sl_ref, out_ref, stage, sems):
    count = x_ref.shape[0]
    twice = jnp.concatenate([sh_ref[...], sh_ref[...]], axis=0)

    def put(number):
        start, size = spans(count)[number]
        return pltpu.make_async_copy(stage.at[number % 2, pl.ds(0, size)], out_ref.at[pl.ds(start, size)], sems.at[number % 2])

    numbers = range(len(spans(count)))
    for number in numbers:
        start, size = spans(count)[number]
        place = pl.ds(start, size)
        if number >= 2:
            put(number - 2).wait()
        upper = vh_ref[:, place]
        both = jnp.concatenate([upper, vl_ref[:, place]], axis=0)
        stage[number % 2, :size] = x_ref[place] - (across(both, twice) + across(upper, sl_ref[...]))
        put(number).start()
    for number in numbers[-2:]:
        put(number).wait()


def per_device(peers, line, eigvecs, panels, factors):
    count, width = eigvecs.shape
    columns = panels.shape[2]
    total = columns * line
    per = columns // PIECE
    own = jnp.swapaxes(panels, 1, 2)
    outside = pl.BlockSpec(memory_space=pltpu.HBM)
    inside = pl.BlockSpec(memory_space=pltpu.VMEM)
    pieces = line * per
    held = pl.pallas_call(
        functools.partial(gather_kernel, peers, line),
        out_shape=(
            jax.ShapeDtypeStruct((count, width), F32),
            jax.ShapeDtypeStruct((total, count), BF16),
            jax.ShapeDtypeStruct((total, count), BF16),
            jax.ShapeDtypeStruct((total, width), BF16),
            jax.ShapeDtypeStruct((total, width), BF16),
        ),
        in_specs=[outside] * 3,
        out_specs=(inside,) * 5,
        scratch_shapes=[
            pltpu.VMEM((line, 2, columns, count), F32),
            pltpu.VMEM((total, count), BF16),
            pltpu.VMEM((total, count), BF16),
            pltpu.VMEM((count, width), BF16),
            pltpu.VMEM((count, width), BF16),
            pltpu.VMEM((pieces, PIECE, width), F32),
            pltpu.VMEM((pieces, PIECE, width), F32),
            pltpu.VMEM((pieces, peers - 1, PIECE, width), F32),
            pltpu.VMEM((pieces, peers - 1, PIECE, width), F32),
            pltpu.VMEM((total, width), F32),
            pltpu.VMEM(factors.shape, F32),
            pltpu.SemaphoreType.DMA,
            pltpu.SemaphoreType.DMA,
            pltpu.SemaphoreType.DMA((len(spans(count)),)),
            pltpu.SemaphoreType.DMA((line, 2, per)),
            pltpu.SemaphoreType.DMA((line, 2, per)),
            pltpu.SemaphoreType.DMA((line, 2, per)),
            pltpu.SemaphoreType.DMA((2, pieces)),
            pltpu.SemaphoreType.DMA((2, pieces)),
        ],
        compiler_params=pltpu.CompilerParams(
            collective_id=0, has_side_effects=True, vmem_limit_bytes=30 * 1024 * 1024
        ),
        name="gather_project",
    )(*(pltpu.with_memory_space_constraint(array, pltpu.HBM) for array in (own, eigvecs, factors)))
    return pl.pallas_call(
        update_kernel,
        out_shape=jax.ShapeDtypeStruct((count, width), F32),
        in_specs=[inside] * 5,
        out_specs=outside,
        scratch_shapes=[pltpu.VMEM((2, DEPTH, width), F32), pltpu.SemaphoreType.DMA((2,))],
        compiler_params=pltpu.CompilerParams(vmem_limit_bytes=24 * 1024 * 1024),
        name="update",
    )(*held)


def solution(mesh):
    return jax.shard_map(
        functools.partial(per_device, mesh.shape["row"], mesh.shape["col"]),
        mesh=mesh,
        in_specs=(P("row", "col"), P(None, "row", "col"), P()),
        out_specs=P("row", "col"),
        check_vma=False,
    )
```

```python
import functools

import jax
import jax.numpy as jnp
from jax import lax
from jax.experimental import pallas as pl
from jax.experimental.pallas import tpu as pltpu
from jax.sharding import PartitionSpec as P

MESH = pl.DeviceIdType.MESH
PIECE = 16
DEPTH = 768
F32 = jnp.float32
BF16 = jnp.bfloat16


def halves(value):
    high = value.astype(BF16)
    return high, (value - high.astype(F32)).astype(BF16)


def rows_by(left, right):
    return lax.dot_general(left, right, (((1,), (1,)), ((), ())), preferred_element_type=F32)


def plain(left, right):
    return lax.dot_general(left, right, (((1,), (0,)), ((), ())), preferred_element_type=F32)


def across(left, right):
    return lax.dot_general(left, right, (((0,), (0,)), ((), ())), preferred_element_type=F32)


def spans(count):
    return [(start, min(DEPTH, count - start)) for start in range(0, count, DEPTH)]


def exact(left, right):
    return jnp.dot(left, right, precision=lax.Precision.HIGHEST, preferred_element_type=F32)


def gather_kernel(
    peers, line, own_ref, x_ref, factors_hbm, x1, vh1, vl1, sh_ref, sl_ref,
    vt, vh0, vl0, xh, xl, part0, part1, part2, got0, got1, got2, scaled, final, factors_ref,
    own_sem, factors_sem, x_sem, left_sem, right_sem, recv_sem, put_sem, got_sem,
):
    row, col = lax.axis_index("row"), lax.axis_index("col")
    columns, count = own_ref.shape[1:]
    per = columns // PIECE
    early = per // 2
    full, rest = count // DEPTH, count % DEPTH
    highs, lows = (vh0, vh1), (vl0, vl1)
    parts, gots = (part0, part1, part2), (got0, got1, got2)

    own_copy = pltpu.make_async_copy(own_ref, vt.at[col], own_sem)
    factors_copy = pltpu.make_async_copy(factors_hbm, factors_ref, factors_sem)

    def fetch(number):
        start, size = spans(count)[number]
        place = pl.ds(start, size)
        return pltpu.make_async_copy(x_ref.at[place], x1.at[place], x_sem.at[number])

    barrier = pltpu.get_barrier_semaphore()
    for offset in range(1, peers):
        pl.semaphore_signal(barrier, inc=1, device_id=(lax.rem(row + offset, peers), col), device_id_type=MESH)

    @pl.when(col > 0)
    def _():
        pl.semaphore_signal(barrier, inc=1, device_id=(row, col - 1), device_id_type=MESH)

    @pl.when(col < line - 1)
    def _():
        pl.semaphore_signal(barrier, inc=1, device_id=(row, col + 1), device_id_type=MESH)

    own_copy.start()
    for number in range(len(spans(count))):
        fetch(number).start()
    factors_copy.start()
    pl.semaphore_wait(barrier, peers - 1 + jnp.where(col > 0, 1, 0) + jnp.where(col < line - 1, 1, 0))

    def move(source, origin, panel, half, sems, away, target):
        place = pl.ds(pl.multiple_of(half * PIECE, PIECE), PIECE)
        return pltpu.make_async_remote_copy(
            src_ref=source.at[panel, place],
            dst_ref=vt.at[origin, panel, place],
            send_sem=sems.at[away, panel, half],
            recv_sem=recv_sem.at[origin, panel, half],
            device_id=(row, target),
            device_id_type=MESH,
        )

    def own_left(panel, half):
        return move(own_ref, col, panel, half, left_sem, 0, col - 1)

    def own_right(panel, half):
        return move(own_ref, col, panel, half, right_sem, 0, col + 1)

    firsts = [(0, half) for half in range(per)] + [(1, half) for half in range(early)]
    lates = [(1, half) for half in range(early, per)]

    for panel, half in firsts:
        @pl.when(col > 0)
        def _():
            own_left(panel, half).start()

        @pl.when(col < line - 1)
        def _():
            own_right(panel, half).start()

    for panel, half in lates:
        @pl.when(col == line - 1)
        def _():
            own_left(panel, half).start()

        @pl.when(col == 0)
        def _():
            own_right(panel, half).start()

    for number, (start, size) in enumerate(spans(count)):
        fetch(number).wait()

        @pl.loop(0, size // 64)
        def _(block):
            place = pl.ds(pl.multiple_of(start + block * 64, 64), 64)
            high, low = halves(x1[place])
            xh[place] = high
            xl[place] = low

    own_copy.wait()
    factors_copy.wait()

    def spread(kind, index):
        @pl.loop(1, peers)
        def _(offset):
            pltpu.make_async_remote_copy(
                src_ref=parts[kind].at[index],
                dst_ref=gots[kind].at[index, offset - 1],
                send_sem=put_sem.at[kind, index],
                recv_sem=got_sem.at[kind, index],
                device_id=(lax.rem(row + offset, peers), col),
                device_id_type=MESH,
            ).start()

    def process(origin, panel, half, pieces, project=True, overlap=False):
        index = origin * per + half
        size = pieces * PIECE
        place = pl.ds(pl.multiple_of(index * PIECE, PIECE), size)
        source = pl.ds(pl.multiple_of(half * PIECE, PIECE), size)

        def add(kind, value):
            for piece in range(pieces):
                parts[kind][index + piece] += value[piece * PIECE : (piece + 1) * PIECE]

        for piece in range(pieces):
            if project:
                parts[panel][index + piece] = jnp.zeros(parts[panel].shape[1:], F32)
            if overlap:
                parts[2][index + piece] = jnp.zeros(parts[2].shape[1:], F32)

        def block(lanes):
            if project:
                high, low = halves(vt[origin, panel, source, lanes])
                highs[panel][place, lanes] = high
                lows[panel][place, lanes] = low
            else:
                high, low = highs[panel][place, lanes], lows[panel][place, lanes]
            both = jnp.concatenate([high, low], axis=0)
            if project:
                first = plain(both, xh[lanes])
                add(panel, first[:size] + first[size:] + plain(high, xl[lanes]))
            if overlap:
                third = rows_by(both, vh0[:, lanes])
                add(2, third[:size] + third[size:] + rows_by(high, vl0[:, lanes]))

        @pl.loop(0, full)
        def _(number):
            block(pl.ds(pl.multiple_of(number * DEPTH, DEPTH), DEPTH))

        if rest:
            block(pl.ds(full * DEPTH, rest))

        for piece in range(pieces):
            if project:
                spread(panel, index + piece)
            if overlap:
                spread(2, index + piece)

    def sides(away, act):
        @pl.when(col + away < line)
        def _():
            act(col + away)

        @pl.when(col - away >= 0)
        def _():
            act(col - away)

    def receive(panel, away, half):
        right, left = col + away, col - away

        @pl.when(right < line)
        def _():
            move(own_ref, right, panel, half, left_sem, away, col).wait_recv()

            @pl.when(col > 0)
            def _():
                move(vt.at[right], right, panel, half, left_sem, away, col - 1).start()

        @pl.when(left >= 0)
        def _():
            move(own_ref, left, panel, half, right_sem, away, col).wait_recv()

            @pl.when(col < line - 1)
            def _():
                move(vt.at[left], left, panel, half, right_sem, away, col + 1).start()

    def receive_all(panel, away):
        for half in range(per):
            receive(panel, away, half)

    def gather_sum(kind, index):
        got = gots[kind]
        pltpu.make_async_copy(got.at[index], got.at[index], got_sem.at[kind, index]).wait()
        total = parts[kind][index]
        for offset in range(peers - 1):
            total = total + got[index, offset]
        return total

    process(col, 0, 0, per)

    @pl.loop(1, line)
    def _(away):
        receive_all(0, away)

        for panel, half in lates:
            @pl.when(jnp.logical_and(col + away == line - 1, col > 0))
            def _():
                own_left(panel, half).start()

            @pl.when(jnp.logical_and(col - away == 0, col < line - 1))
            def _():
                own_right(panel, half).start()

        sides(away, lambda origin: process(origin, 0, 0, per))

        @pl.when(away == 1)
        def _():
            process(col, 1, 0, per)

    def apply_first():
        @pl.loop(0, line * per)
        def _(index):
            scaled[pl.ds(pl.multiple_of(index * PIECE, PIECE), PIECE)] = gather_sum(0, index)

        value = exact(factors_ref[0], scaled[...])
        scaled[...] = value
        high, low = halves(value)
        sh_ref[...] = high
        sl_ref[...] = low

        def block(lanes):
            upper, lower = vh0[:, lanes], vl0[:, lanes]
            both = jnp.concatenate([upper, lower], axis=0)
            twice = jnp.concatenate([sh_ref[...], sh_ref[...]], axis=0)
            x1[lanes] = x1[lanes] - (across(both, twice) + across(upper, sl_ref[...]))

        @pl.loop(0, full)
        def _(number):
            block(pl.ds(pl.multiple_of(number * DEPTH, DEPTH), DEPTH))

        if rest:
            block(pl.ds(full * DEPTH, rest))

        process(col, 1, 0, per, project=False, overlap=True)

    for away in range(1, line - 1):
        receive_all(1, away)
        if away == 1:
            sides(away, lambda origin: process(origin, 1, 0, per))
            apply_first()
            sides(away, lambda origin: process(origin, 1, 0, per, project=False, overlap=True))
        else:
            sides(away, lambda origin: process(origin, 1, 0, per, overlap=True))
    if line == 2:
        apply_first()

    def settle(index):
        corrected = gather_sum(1, index) - exact(gather_sum(2, index), scaled[...])
        final[pl.ds(pl.multiple_of(index * PIECE, PIECE), PIECE)] = corrected

    @pl.loop(0, line)
    def _(origin):
        @pl.when(jnp.logical_and(origin - col < line - 1, col - origin < line - 1))
        def _():
            @pl.loop(0, per)
            def _(half):
                settle(origin * per + half)

    for half in range(per):
        receive(1, line - 1, half)
        sides(line - 1, lambda origin: process(origin, 1, half, 1, overlap=True))
        if half < per - 1:
            sides(line - 1, lambda origin: settle(origin * per + half))
    sides(line - 1, lambda origin: settle(origin * per + per - 1))

    high, low = halves(exact(factors_ref[1], final[...]))
    sh_ref[...] = high
    sl_ref[...] = low

    for panel in range(2):
        for half in range(per):
            @pl.when(col > 0)
            def _():
                own_left(panel, half).wait_send()

            @pl.when(col < line - 1)
            def _():
                own_right(panel, half).wait_send()

        @pl.loop(1, line)
        def _(away):
            @pl.loop(0, per)
            def _(half):
                @pl.when(jnp.logical_and(col + away < line, col > 0))
                def _():
                    move(own_ref, col + away, panel, half, left_sem, away, col - 1).wait_send()

                @pl.when(jnp.logical_and(col - away >= 0, col < line - 1))
                def _():
                    move(own_ref, col - away, panel, half, right_sem, away, col + 1).wait_send()

    for kind in range(3):
        got = gots[kind]

        @pl.loop(0, line * per)
        def _(index):
            pltpu.make_async_copy(got.at[index], got.at[index], put_sem.at[kind, index]).wait()


def update_kernel(x_ref, vh_ref, vl_ref, sh_ref, sl_ref, out_ref, stage, sems):
    count = x_ref.shape[0]
    twice = jnp.concatenate([sh_ref[...], sh_ref[...]], axis=0)

    def put(number):
        start, size = spans(count)[number]
        return pltpu.make_async_copy(stage.at[number % 2, pl.ds(0, size)], out_ref.at[pl.ds(start, size)], sems.at[number % 2])

    numbers = range(len(spans(count)))
    for number in numbers:
        start, size = spans(count)[number]
        place = pl.ds(start, size)
        if number >= 2:
            put(number - 2).wait()
        upper = vh_ref[:, place]
        both = jnp.concatenate([upper, vl_ref[:, place]], axis=0)
        stage[number % 2, :size] = x_ref[place] - (across(both, twice) + across(upper, sl_ref[...]))
        put(number).start()
    for number in numbers[-2:]:
        put(number).wait()


def per_device(peers, line, eigvecs, panels, factors):
    count, width = eigvecs.shape
    columns = panels.shape[2]
    total = columns * line
    per = columns // PIECE
    own = jnp.swapaxes(panels, 1, 2)
    outside = pl.BlockSpec(memory_space=pltpu.HBM)
    inside = pl.BlockSpec(memory_space=pltpu.VMEM)
    pieces = line * per
    held = pl.pallas_call(
        functools.partial(gather_kernel, peers, line),
        out_shape=(
            jax.ShapeDtypeStruct((count, width), F32),
            jax.ShapeDtypeStruct((total, count), BF16),
            jax.ShapeDtypeStruct((total, count), BF16),
            jax.ShapeDtypeStruct((total, width), BF16),
            jax.ShapeDtypeStruct((total, width), BF16),
        ),
        in_specs=[outside] * 3,
        out_specs=(inside,) * 5,
        scratch_shapes=[
            pltpu.VMEM((line, 2, columns, count), F32),
            pltpu.VMEM((total, count), BF16),
            pltpu.VMEM((total, count), BF16),
            pltpu.VMEM((count, width), BF16),
            pltpu.VMEM((count, width), BF16),
            pltpu.VMEM((pieces, PIECE, width), F32),
            pltpu.VMEM((pieces, PIECE, width), F32),
            pltpu.VMEM((pieces, PIECE, total), F32),
            pltpu.VMEM((pieces, peers - 1, PIECE, width), F32),
            pltpu.VMEM((pieces, peers - 1, PIECE, width), F32),
            pltpu.VMEM((pieces, peers - 1, PIECE, total), F32),
            pltpu.VMEM((total, width), F32),
            pltpu.VMEM((total, width), F32),
            pltpu.VMEM(factors.shape, F32),
            pltpu.SemaphoreType.DMA,
            pltpu.SemaphoreType.DMA,
            pltpu.SemaphoreType.DMA((len(spans(count)),)),
            pltpu.SemaphoreType.DMA((line, 2, per)),
            pltpu.SemaphoreType.DMA((line, 2, per)),
            pltpu.SemaphoreType.DMA((line, 2, per)),
            pltpu.SemaphoreType.DMA((3, pieces)),
            pltpu.SemaphoreType.DMA((3, pieces)),
        ],
        compiler_params=pltpu.CompilerParams(
            collective_id=0, has_side_effects=True, vmem_limit_bytes=30 * 1024 * 1024
        ),
        name="gather_project",
    )(*(pltpu.with_memory_space_constraint(array, pltpu.HBM) for array in (own, eigvecs, factors)))
    return pl.pallas_call(
        update_kernel,
        out_shape=jax.ShapeDtypeStruct((count, width), F32),
        in_specs=[inside] * 5,
        out_specs=outside,
        scratch_shapes=[pltpu.VMEM((2, DEPTH, width), F32), pltpu.SemaphoreType.DMA((2,))],
        compiler_params=pltpu.CompilerParams(vmem_limit_bytes=24 * 1024 * 1024),
        name="update",
    )(*held)


def solution(mesh):
    return jax.shard_map(
        functools.partial(per_device, mesh.shape["row"], mesh.shape["col"]),
        mesh=mesh,
        in_specs=(P("row", "col"), P(None, "row", "col"), P()),
        out_specs=P("row", "col"),
        check_vma=False,
    )
```

```python
import functools

import jax
import jax.numpy as jnp
from jax import lax
from jax.experimental import pallas as pl
from jax.experimental.pallas import tpu as pltpu
from jax.sharding import PartitionSpec as P

MESH = pl.DeviceIdType.MESH
PIECE = 16
DEPTH = 768
F32 = jnp.float32
BF16 = jnp.bfloat16


def halves(value):
    high = value.astype(BF16)
    return high, (value - high.astype(F32)).astype(BF16)


def rows_by(left, right):
    return lax.dot_general(left, right, (((1,), (1,)), ((), ())), preferred_element_type=F32)


def plain(left, right):
    return lax.dot_general(left, right, (((1,), (0,)), ((), ())), preferred_element_type=F32)


def across(left, right):
    return lax.dot_general(left, right, (((0,), (0,)), ((), ())), preferred_element_type=F32)


def spans(count):
    return [(start, min(DEPTH, count - start)) for start in range(0, count, DEPTH)]


def exact(left, right):
    return jnp.dot(left, right, precision=lax.Precision.HIGHEST, preferred_element_type=F32)


def gather_kernel(
    peers, line, own_ref, x_ref, factors_hbm, x1, vh1, vl1, sh_ref, sl_ref,
    vt, vh0, vl0, xh, xl, part0, part1, part2, got0, got1, got2, scaled, final, gram, factors_ref,
    own_sem, factors_sem, x_sem, left_sem, right_sem, recv_sem, put_sem, got_sem,
):
    row, col = lax.axis_index("row"), lax.axis_index("col")
    columns, count = own_ref.shape[1:]
    per = columns // PIECE
    early = per // 2
    full, rest = count // DEPTH, count % DEPTH
    highs, lows = (vh0, vh1), (vl0, vl1)
    parts, gots = (part0, part1, part2), (got0, got1, got2)

    own_copy = pltpu.make_async_copy(own_ref, vt.at[col], own_sem)
    factors_copy = pltpu.make_async_copy(factors_hbm, factors_ref, factors_sem)

    def fetch(number):
        start, size = spans(count)[number]
        place = pl.ds(start, size)
        return pltpu.make_async_copy(x_ref.at[place], x1.at[place], x_sem.at[number])

    barrier = pltpu.get_barrier_semaphore()
    for offset in range(1, peers):
        pl.semaphore_signal(barrier, inc=1, device_id=(lax.rem(row + offset, peers), col), device_id_type=MESH)

    @pl.when(col > 0)
    def _():
        pl.semaphore_signal(barrier, inc=1, device_id=(row, col - 1), device_id_type=MESH)

    @pl.when(col < line - 1)
    def _():
        pl.semaphore_signal(barrier, inc=1, device_id=(row, col + 1), device_id_type=MESH)

    own_copy.start()
    for number in range(len(spans(count))):
        fetch(number).start()
    factors_copy.start()
    pl.semaphore_wait(barrier, peers - 1 + jnp.where(col > 0, 1, 0) + jnp.where(col < line - 1, 1, 0))

    def move(source, origin, panel, half, sems, away, target):
        place = pl.ds(pl.multiple_of(half * PIECE, PIECE), PIECE)
        return pltpu.make_async_remote_copy(
            src_ref=source.at[panel, place],
            dst_ref=vt.at[origin, panel, place],
            send_sem=sems.at[away, panel, half],
            recv_sem=recv_sem.at[origin, panel, half],
            device_id=(row, target),
            device_id_type=MESH,
        )

    def own_left(panel, half):
        return move(own_ref, col, panel, half, left_sem, 0, col - 1)

    def own_right(panel, half):
        return move(own_ref, col, panel, half, right_sem, 0, col + 1)

    firsts = [(0, half) for half in range(per)] + [(1, half) for half in range(early)]
    lates = [(1, half) for half in range(early, per)]

    for panel, half in firsts:
        @pl.when(col > 0)
        def _():
            own_left(panel, half).start()

        @pl.when(col < line - 1)
        def _():
            own_right(panel, half).start()

    for panel, half in lates:
        @pl.when(col == line - 1)
        def _():
            own_left(panel, half).start()

        @pl.when(col == 0)
        def _():
            own_right(panel, half).start()

    for number, (start, size) in enumerate(spans(count)):
        fetch(number).wait()

        @pl.loop(0, size // 64)
        def _(block):
            place = pl.ds(pl.multiple_of(start + block * 64, 64), 64)
            high, low = halves(x1[place])
            xh[place] = high
            xl[place] = low

    own_copy.wait()
    factors_copy.wait()

    def spread(kind, index):
        @pl.loop(1, peers)
        def _(offset):
            pltpu.make_async_remote_copy(
                src_ref=parts[kind].at[index],
                dst_ref=gots[kind].at[index, offset - 1],
                send_sem=put_sem.at[kind, index],
                recv_sem=got_sem.at[kind, index],
                device_id=(lax.rem(row + offset, peers), col),
                device_id_type=MESH,
            ).start()

    def process(origin, panel, half, pieces, project=True, overlap=False):
        index = origin * per + half
        size = pieces * PIECE
        place = pl.ds(pl.multiple_of(index * PIECE, PIECE), size)
        source = pl.ds(pl.multiple_of(half * PIECE, PIECE), size)

        def add(kind, value):
            for piece in range(pieces):
                parts[kind][index + piece] += value[piece * PIECE : (piece + 1) * PIECE]

        for piece in range(pieces):
            if project:
                parts[panel][index + piece] = jnp.zeros(parts[panel].shape[1:], F32)
            if overlap:
                parts[2][index + piece] = jnp.zeros(parts[2].shape[1:], F32)

        def block(lanes):
            if project:
                high, low = halves(vt[origin, panel, source, lanes])
                highs[panel][place, lanes] = high
                lows[panel][place, lanes] = low
            else:
                high, low = highs[panel][place, lanes], lows[panel][place, lanes]
            both = jnp.concatenate([high, low], axis=0)
            if project:
                first = plain(both, xh[lanes])
                add(panel, first[:size] + first[size:] + plain(high, xl[lanes]))
            if overlap:
                third = rows_by(both, vh0[:, lanes])
                add(2, third[:size] + third[size:] + rows_by(high, vl0[:, lanes]))

        @pl.loop(0, full)
        def _(number):
            block(pl.ds(pl.multiple_of(number * DEPTH, DEPTH), DEPTH))

        if rest:
            block(pl.ds(full * DEPTH, rest))

        for piece in range(pieces):
            if project:
                spread(panel, index + piece)
            if overlap:
                spread(2, index + piece)

    def sides(away, act):
        @pl.when(col + away < line)
        def _():
            act(col + away)

        @pl.when(col - away >= 0)
        def _():
            act(col - away)

    def receive(panel, away, half):
        right, left = col + away, col - away

        @pl.when(right < line)
        def _():
            move(own_ref, right, panel, half, left_sem, away, col).wait_recv()

            @pl.when(col > 0)
            def _():
                move(vt.at[right], right, panel, half, left_sem, away, col - 1).start()

        @pl.when(left >= 0)
        def _():
            move(own_ref, left, panel, half, right_sem, away, col).wait_recv()

            @pl.when(col < line - 1)
            def _():
                move(vt.at[left], left, panel, half, right_sem, away, col + 1).start()

    def receive_all(panel, away):
        for half in range(per):
            receive(panel, away, half)

    def gather_sum(kind, index):
        got = gots[kind]
        pltpu.make_async_copy(got.at[index], got.at[index], got_sem.at[kind, index]).wait()
        total = parts[kind][index]
        for offset in range(peers - 1):
            total = total + got[index, offset]
        return total

    process(col, 0, 0, per)

    @pl.loop(1, line)
    def _(away):
        receive_all(0, away)

        for panel, half in lates:
            @pl.when(jnp.logical_and(col + away == line - 1, col > 0))
            def _():
                own_left(panel, half).start()

            @pl.when(jnp.logical_and(col - away == 0, col < line - 1))
            def _():
                own_right(panel, half).start()

        sides(away, lambda origin: process(origin, 0, 0, per))

        @pl.when(away == 1)
        def _():
            process(col, 1, 0, per)

    def apply_first():
        @pl.loop(0, line * per)
        def _(index):
            scaled[pl.ds(pl.multiple_of(index * PIECE, PIECE), PIECE)] = gather_sum(0, index)

        value = exact(factors_ref[0], scaled[...])
        scaled[...] = value
        high, low = halves(value)
        sh_ref[...] = high
        sl_ref[...] = low

        def block(lanes):
            upper, lower = vh0[:, lanes], vl0[:, lanes]
            both = jnp.concatenate([upper, lower], axis=0)
            twice = jnp.concatenate([sh_ref[...], sh_ref[...]], axis=0)
            x1[lanes] = x1[lanes] - (across(both, twice) + across(upper, sl_ref[...]))

        @pl.loop(0, full)
        def _(number):
            block(pl.ds(pl.multiple_of(number * DEPTH, DEPTH), DEPTH))

        if rest:
            block(pl.ds(full * DEPTH, rest))

        process(col, 1, 0, per, project=False, overlap=True)

    for away in range(1, line - 1):
        receive_all(1, away)
        if away == 1:
            sides(away, lambda origin: process(origin, 1, 0, per))
            apply_first()
            sides(away, lambda origin: process(origin, 1, 0, per, project=False, overlap=True))
        else:
            sides(away, lambda origin: process(origin, 1, 0, per, overlap=True))
    if line == 2:
        apply_first()

    def settle(index):
        place = pl.ds(pl.multiple_of(index * PIECE, PIECE), PIECE)
        final[place] = gather_sum(1, index)
        gram[place] = gather_sum(2, index)

    @pl.loop(0, line)
    def _(origin):
        @pl.when(jnp.logical_and(origin - col < line - 1, col - origin < line - 1))
        def _():
            @pl.loop(0, per)
            def _(half):
                settle(origin * per + half)

    for half in range(per):
        receive(1, line - 1, half)
        sides(line - 1, lambda origin: process(origin, 1, half, 1, overlap=True))
    for half in range(per):
        sides(line - 1, lambda origin: settle(origin * per + half))

    projection = final[...] - exact(gram[...], scaled[...])
    high, low = halves(exact(factors_ref[1], projection))
    sh_ref[...] = high
    sl_ref[...] = low

    for panel in range(2):
        for half in range(per):
            @pl.when(col > 0)
            def _():
                own_left(panel, half).wait_send()

            @pl.when(col < line - 1)
            def _():
                own_right(panel, half).wait_send()

        @pl.loop(1, line)
        def _(away):
            @pl.loop(0, per)
            def _(half):
                @pl.when(jnp.logical_and(col + away < line, col > 0))
                def _():
                    move(own_ref, col + away, panel, half, left_sem, away, col - 1).wait_send()

                @pl.when(jnp.logical_and(col - away >= 0, col < line - 1))
                def _():
                    move(own_ref, col - away, panel, half, right_sem, away, col + 1).wait_send()

    for kind in range(3):
        got = gots[kind]

        @pl.loop(0, line * per)
        def _(index):
            pltpu.make_async_copy(got.at[index], got.at[index], put_sem.at[kind, index]).wait()


def update_kernel(x_ref, vh_ref, vl_ref, sh_ref, sl_ref, out_ref, stage, sems):
    count = x_ref.shape[0]
    twice = jnp.concatenate([sh_ref[...], sh_ref[...]], axis=0)

    def put(number):
        start, size = spans(count)[number]
        return pltpu.make_async_copy(stage.at[number % 2, pl.ds(0, size)], out_ref.at[pl.ds(start, size)], sems.at[number % 2])

    numbers = range(len(spans(count)))
    for number in numbers:
        start, size = spans(count)[number]
        place = pl.ds(start, size)
        if number >= 2:
            put(number - 2).wait()
        upper = vh_ref[:, place]
        both = jnp.concatenate([upper, vl_ref[:, place]], axis=0)
        stage[number % 2, :size] = x_ref[place] - (across(both, twice) + across(upper, sl_ref[...]))
        put(number).start()
    for number in numbers[-2:]:
        put(number).wait()


def per_device(peers, line, eigvecs, panels, factors):
    count, width = eigvecs.shape
    columns = panels.shape[2]
    total = columns * line
    per = columns // PIECE
    own = jnp.swapaxes(panels, 1, 2)
    outside = pl.BlockSpec(memory_space=pltpu.HBM)
    inside = pl.BlockSpec(memory_space=pltpu.VMEM)
    pieces = line * per
    held = pl.pallas_call(
        functools.partial(gather_kernel, peers, line),
        out_shape=(
            jax.ShapeDtypeStruct((count, width), F32),
            jax.ShapeDtypeStruct((total, count), BF16),
            jax.ShapeDtypeStruct((total, count), BF16),
            jax.ShapeDtypeStruct((total, width), BF16),
            jax.ShapeDtypeStruct((total, width), BF16),
        ),
        in_specs=[outside] * 3,
        out_specs=(inside,) * 5,
        scratch_shapes=[
            pltpu.VMEM((line, 2, columns, count), F32),
            pltpu.VMEM((total, count), BF16),
            pltpu.VMEM((total, count), BF16),
            pltpu.VMEM((count, width), BF16),
            pltpu.VMEM((count, width), BF16),
            pltpu.VMEM((pieces, PIECE, width), F32),
            pltpu.VMEM((pieces, PIECE, width), F32),
            pltpu.VMEM((pieces, PIECE, total), F32),
            pltpu.VMEM((pieces, peers - 1, PIECE, width), F32),
            pltpu.VMEM((pieces, peers - 1, PIECE, width), F32),
            pltpu.VMEM((pieces, peers - 1, PIECE, total), F32),
            pltpu.VMEM((total, width), F32),
            pltpu.VMEM((total, width), F32),
            pltpu.VMEM((total, total), F32),
            pltpu.VMEM(factors.shape, F32),
            pltpu.SemaphoreType.DMA,
            pltpu.SemaphoreType.DMA,
            pltpu.SemaphoreType.DMA((len(spans(count)),)),
            pltpu.SemaphoreType.DMA((line, 2, per)),
            pltpu.SemaphoreType.DMA((line, 2, per)),
            pltpu.SemaphoreType.DMA((line, 2, per)),
            pltpu.SemaphoreType.DMA((3, pieces)),
            pltpu.SemaphoreType.DMA((3, pieces)),
        ],
        compiler_params=pltpu.CompilerParams(
            collective_id=0, has_side_effects=True, vmem_limit_bytes=30 * 1024 * 1024
        ),
        name="gather_project",
    )(*(pltpu.with_memory_space_constraint(array, pltpu.HBM) for array in (own, eigvecs, factors)))
    return pl.pallas_call(
        update_kernel,
        out_shape=jax.ShapeDtypeStruct((count, width), F32),
        in_specs=[inside] * 5,
        out_specs=outside,
        scratch_shapes=[pltpu.VMEM((2, DEPTH, width), F32), pltpu.SemaphoreType.DMA((2,))],
        compiler_params=pltpu.CompilerParams(vmem_limit_bytes=24 * 1024 * 1024),
        name="update",
    )(*held)


def solution(mesh):
    return jax.shard_map(
        functools.partial(per_device, mesh.shape["row"], mesh.shape["col"]),
        mesh=mesh,
        in_specs=(P("row", "col"), P(None, "row", "col"), P()),
        out_specs=P("row", "col"),
        check_vma=False,
    )
```
